32 devices in a mesh: cycle: 2 (over x), gx: 8 (over z, y), gy: 2 (over core).
Axes of the slice: x: 2, y: 2, z: 4, core: 2. Of those that a mesh axis runs over, the one named last changes fastest.
Arguments:
- stored_thermal_state: float32 [128, 64, 1024], P(('cycle', 'gx'), 'gy'), parts along dimension 0, may hold values from 0.2 to 1
- substance_label: int32 [64, 64, 1024], P('gx', 'gy'), may hold values from 0 to 7
- convection_flag: int32 [64, 64, 1024], P('gx', 'gy'), may hold values 0 or 1
- adjoint_source: float32 [128, 64, 1024], P(('cycle', 'gx'), 'gy'), parts along dimension 0, may hold values from -200 to 200
- zero_kelvin_diffusivity: float32 [8], replicated, may hold values from 0.5 to 4
- thermal_coefficient: float32 [8], replicated, may hold values from -0.4 to 0.6
- thermal_storage_rate: float32 [8], replicated, may hold values from 0.3 to 3
Outputs:
- adjoint: float32 [128, 64, 1024], P(('cycle', 'gx'), 'gy'), parts along dimension 0
- residual: float32 [128, 64, 1024], P(('cycle', 'gx'), 'gy'), parts along dimension 0
The draws below stay inside these ranges and needn't reach their ends.
There are 2 independent parts, one for each index of `cycle`. The reference program is written for one: setup_inputs(seed, part) draws one part's arguments, and reference() takes and returns one part's arrays. A program takes and returns all parts, laid end to end along the dimension named above; an argument that names none is the same for every part. Nothing has to cross between parts.
All inputs are finite; a program needn't handle non-finite values. No bound on the sum of `convection_flag` on one device may be relied on, other than what follows from the above.
Results may differ from the reference program's by a relative error of at most 0.00025.
Values sent between devices are 32-bit elements; how exact they have to be, the bound alone decides.
A program may use at most 64 MiB of HBM per device.

```python
import math
import jax
import jax.numpy as jnp

VOXELS_THIRD_AXIS = 1024
MATS = 8
ITERS = 4
VOXELS_ROW_AXIS = 64
VOXELS_COL_AXIS = 64


def draw_adjoint_source(key, part):
    key = jax.random.fold_in(key, 7)
    first, second, third = jax.random.split(key, 3)
    shape = (VOXELS_ROW_AXIS, VOXELS_COL_AXIS, VOXELS_THIRD_AXIS)
    plane = jnp.exp(jax.random.uniform(second, (VOXELS_ROW_AXIS, 1, 1), jnp.float32) * math.log(10.0)) / math.sqrt(10.0)
    row = jnp.exp(jax.random.uniform(third, (1, VOXELS_COL_AXIS, 1), jnp.float32) * math.log(10.0)) / math.sqrt(10.0)
    ramp = 1.0 + 2.0 * jnp.arange(VOXELS_ROW_AXIS, dtype=jnp.float32).reshape(VOXELS_ROW_AXIS, 1, 1) / VOXELS_ROW_AXIS
    rough = jnp.clip(jax.random.normal(first, shape, jnp.float32), -6.0, 6.0)
    return rough * plane * row * ramp


def set_ends(entries, key, low, largest):
    spot = [jax.random.randint(jax.random.fold_in(key, axis), (), 0, length) for axis, length in enumerate(entries.shape)]
    longest = entries.shape.index(max(entries.shape))
    next_to = spot[:longest] + [(spot[longest] + 1) % entries.shape[longest]] + spot[longest + 1:]
    return entries.at[tuple(spot)].set(low).at[tuple(next_to)].set(largest)


def steps_of(key, shape, pieces, least, largest):
    def one(position, shards_of):
        heights = jax.random.uniform(jax.random.fold_in(jax.random.fold_in(key, 6), position), (shards_of,), jnp.float32, least / len(pieces), largest / len(pieces))
        return jnp.repeat(jnp.exp(heights), shape[position] // shards_of).reshape((-1,) + (1,) * (len(shape) - position - 1))

    factor_of = one(*pieces[0])
    for cut in pieces[1:]:
        factor_of = factor_of * one(*cut)
    return factor_of


def setup_inputs(seed: int = 0, part: int = 0) -> dict:
    keys = jax.random.split(jax.random.key(seed), 8)
    part_keys = jax.random.split(jax.random.fold_in(keys[7], part), 8)
    stored_thermal_state = jnp.clip(0.2 + 0.8 * jax.random.uniform(part_keys[0], (VOXELS_ROW_AXIS, VOXELS_COL_AXIS, VOXELS_THIRD_AXIS), jnp.float32) ** steps_of(part_keys[0], (VOXELS_ROW_AXIS, VOXELS_COL_AXIS, VOXELS_THIRD_AXIS), ((0, 8), (1, 2)), -0.2, 0.2), 0.2, 1.0)
    substance_label = set_ends(jax.random.randint(keys[1], (VOXELS_ROW_AXIS, VOXELS_COL_AXIS, VOXELS_THIRD_AXIS), 0, MATS), jax.random.fold_in(keys[1], 1), 0, MATS - 1).astype(jnp.int32)
    convection_flag = set_ends((jax.random.randint(keys[2], (VOXELS_ROW_AXIS, VOXELS_COL_AXIS, VOXELS_THIRD_AXIS), 0, 4) < 1).astype(jnp.int32), jax.random.fold_in(keys[2], 1), 0, 1)
    adjoint_source = draw_adjoint_source(jax.random.fold_in(jax.random.fold_in(keys[7], part), 71), part)
    zero_kelvin_diffusivity = jnp.clip(jnp.exp(jax.random.uniform(keys[4], (MATS,), jnp.float32, math.log(0.5), math.log(4.0))), 0.5, 4.0)
    thermal_coefficient = jnp.clip(jax.random.uniform(keys[5], (MATS,), jnp.float32, -0.4, 0.6), -0.4, 0.6)
    thermal_storage_rate = jnp.clip(jnp.exp(jax.random.uniform(keys[6], (MATS,), jnp.float32, math.log(0.3), math.log(3.0))), 0.3, 3.0)
    return dict(stored_thermal_state=stored_thermal_state, substance_label=substance_label, convection_flag=convection_flag, adjoint_source=adjoint_source, zero_kelvin_diffusivity=zero_kelvin_diffusivity, thermal_coefficient=thermal_coefficient, thermal_storage_rate=thermal_storage_rate)


HCOOL = 1.5


def harmonic(near, far):
    return 2.0 * near * far / (near + far)


def beside_all(field):
    padded = jnp.pad(field, 1)
    return (padded[:-2, 1:-1, 1:-1], padded[2:, 1:-1, 1:-1],
            padded[1:-1, :-2, 1:-1], padded[1:-1, 2:, 1:-1],
            padded[1:-1, 1:-1, :-2], padded[1:-1, 1:-1, 2:])


def operate(field, faces, diag):
    result = diag * field
    for face, near in zip(faces, beside_all(field)):
        result = result - face * near
    return result


def reference(stored_thermal_state, substance_label, convection_flag, adjoint_source, zero_kelvin_diffusivity, thermal_coefficient, thermal_storage_rate):
    voxel_diffusivity = zero_kelvin_diffusivity[substance_label] * (1.0 + thermal_coefficient[substance_label] * stored_thermal_state)
    base = thermal_storage_rate[substance_label] + HCOOL * convection_flag.astype(jnp.float32)
    faces = tuple(harmonic(voxel_diffusivity, near) for near in beside_all(voxel_diffusivity))
    diag = base
    for face in faces:
        diag = diag + face
    adjoint = jnp.zeros_like(adjoint_source)
    residual = adjoint_source
    pre = residual / diag
    direction = pre
    norm_now = jnp.sum(residual * pre)
    for step in range(ITERS):
        image = operate(direction, faces, diag)
        alpha = norm_now / jnp.sum(direction * image)
        adjoint = adjoint + alpha * direction
        residual = residual - alpha * image
        pre = residual / diag
        norm_next = jnp.sum(residual * pre)
        direction = pre + (norm_next / norm_now) * direction
        norm_now = norm_next
    return adjoint, residual
```

```python
import functools

import jax
import jax.numpy as jnp
from jax import lax
from jax.experimental import pallas as pl
from jax.experimental.pallas import tpu as pltpu
from jax.sharding import PartitionSpec as P

HCOOL = 1.5
STEPS = 4
PAD = 8
MESH = pl.DeviceIdType.MESH


def fold(x):
    total = x[:, :128]
    for lane in range(128, x.shape[1], 128):
        total = total + x[:, lane : lane + 128]
    return total


def harmonic(a, b):
    return 2.0 * a * b / (a + b)


def spread(x):
    return jnp.broadcast_to(jnp.sum(x, axis=(0, 1), keepdims=True), (8, 128))


def kernel(
    ngx, ngy, cuts,
    temp_hbm, label_hbm, flag_hbm, source_hbm, k0_ref, tc_ref, ts_ref,
    adjoint_ref, residual_ref,
    temp, label, flag, source, cond, v0, v1, v2, v3, v4,
    face_row, face_left, face_right, face_down, face_up, inv, diag,
    edge_out, edge_in, part_out, part_in,
    load_sem, row_send, row_recv, edge_send, edge_recv, part_send, part_recv,
):
    rows, cols, depth = temp.shape
    tiles = cols // 8
    gx, gy = lax.axis_index("gx"), lax.axis_index("gy")
    n = ngx * ngy
    me = gx * ngy + gy
    fields = (cond, v0, v1, v2, v3, v4)
    v = fields[1:]
    has_lower, has_upper = gx > 0, gx < ngx - 1

    def peer(offset):
        p = lax.rem(me + offset, n)
        return {"gx": p // ngy, "gy": lax.rem(p, ngy)}

    def load(a, group):
        src, dst = ((temp_hbm, temp), (label_hbm, label), (source_hbm, source), (flag_hbm, flag))[a]
        first, size = ((0, 1), (rows - 1, 1), (1, rows - 2))[group]
        return pltpu.make_async_copy(
            src.at[pl.ds(first, size)], dst.at[pl.ds(first, size)], load_sem.at[a, group]
        )

    order = [(a, g) for a in (0, 1) for g in (0, 1)] + [(a, g) for a in (2, 3) for g in (0, 1)]
    order += [(a, 2) for a in range(4)]
    for a, g in order:
        load(a, g).start()

    barrier = pltpu.get_barrier_semaphore()

    def greet(offset, carry):
        pl.semaphore_signal(barrier, inc=1, device_id=peer(offset), device_id_type=MESH)
        return carry

    lax.fori_loop(1, n, greet, 0)

    zero_row = jnp.zeros((cols, depth), jnp.float32)
    zero_edge = jnp.zeros((8, depth), jnp.float32)

    @pl.when(jnp.logical_not(has_lower))
    def _():
        for field in fields[:-1]:
            field[0, PAD : PAD + cols, :] = zero_row

    @pl.when(jnp.logical_not(has_upper))
    def _():
        for field in fields[:-1]:
            field[rows + 1, PAD : PAD + cols, :] = zero_row

    for field in fields[:-1]:
        for i in range(1, rows + 1):
            field[i, 0:PAD, :] = zero_edge
            field[i, PAD + cols : PAD + cols + 8, :] = zero_edge
    for k in range(STEPS + 1):
        edge_out[k, 0:8, :] = zero_edge
        edge_out[k, 8:16, :] = zero_edge

    width = cols // cuts
    own_edge = jnp.where(gy == 0, PAD + cols - 1, PAD)
    halo_edge = jnp.where(gy == 0, PAD + cols, PAD - 1)

    def row_copy(k, side, c):
        src, dst = ((1, rows + 1), (rows, 0))[side]
        part = pl.ds(PAD + c * width, width)
        return pltpu.make_async_remote_copy(
            src_ref=fields[k].at[src, part, :],
            dst_ref=fields[k].at[dst, part, :],
            send_sem=row_send.at[k, side, c],
            recv_sem=row_recv.at[k, side, c],
            device_id={"gx": gx - 1 if side == 0 else gx + 1},
            device_id_type=MESH,
        )

    def has(side):
        return has_lower if side == 0 else has_upper

    def send_row(k, side, c):
        @pl.when(has(side))
        def _():
            row_copy(k, side, c).start()

    def wait_row(k, end, c):
        @pl.when(has(end))
        def _():
            row_copy(k, 1 - end, c).wait_recv()

    def edge_copy(k, group):
        part = pl.ds(8 * group, 8)
        return pltpu.make_async_remote_copy(
            src_ref=edge_out.at[k, part, :],
            dst_ref=edge_in.at[k, part, :],
            send_sem=edge_send.at[k, group],
            recv_sem=edge_recv.at[k, group],
            device_id={"gy": 1 - gy},
            device_id_type=MESH,
        )

    spots = ([(1, 0), (rows, 1)], [(i, 8 + i - 2) for i in range(2, rows)])

    def send_edge(k, group):
        for i, spot in spots[group]:
            edge_out[k, spot : spot + 1, :] = fields[k][i, pl.ds(own_edge, 1), :]
        edge_copy(k, group).start()

    def wait_edge(k, group):
        edge_copy(k, group).wait_recv()
        for i, spot in spots[group]:
            fields[k][i, pl.ds(halo_edge, 1), :] = edge_in[k, spot : spot + 1, :]

    def table(ref, marks):
        out = jnp.zeros(marks[0].shape, jnp.float32)
        for m, mark in enumerate(marks):
            out = jnp.where(mark, ref[m], out)
        return out

    def conduct(i, t):
        part = pl.ds(8 * t, 8)
        kind = label[i - 1, part, :]
        marks = [kind == m for m in range(k0_ref.shape[0])]
        cond[i, pl.ds(PAD + 8 * t, 8), :] = table(k0_ref, marks) * (
            1.0 + table(tc_ref, marks) * temp[i - 1, part, :]
        )

    def start_row(i, t, end):
        at = PAD + 8 * t
        part = pl.ds(8 * t, 8)
        c = cond[i, pl.ds(at, 8), :]
        lower = harmonic(c, cond[i - 1, pl.ds(at, 8), :])
        upper = harmonic(c, cond[i + 1, pl.ds(at, 8), :])
        left = harmonic(c, cond[i, pl.ds(at - 1, 8), :])
        right = harmonic(c, cond[i, pl.ds(at + 1, 8), :])
        lane = lax.broadcasted_iota(jnp.int32, c.shape, 1)
        down = harmonic(c, jnp.where(lane == 0, 0.0, pltpu.roll(c, 1, 1)))
        up = pltpu.roll(down, depth - 1, 1)
        face_row[i - 1, part, :] = lower
        face_row[i, part, :] = upper
        face_left[i - 1, part, :] = left
        face_right[i - 1, part, :] = right
        face_down[i - 1, part, :] = down
        face_up[i - 1, part, :] = up
        kind = label[i - 1, part, :]
        marks = [kind == m for m in range(k0_ref.shape[0])]
        base = table(ts_ref, marks) + HCOOL * flag[i - 1, part, :].astype(jnp.float32)
        d = base + lower + upper + left + right + down + up
        s = source[i - 1, part, :]
        over = 1.0 / d
        diag[i - 1, part, :] = d
        inv[i - 1, part, :] = over
        z = s * over
        v0[i, pl.ds(at, 8), :] = z
        return fold(z * s)

    def apply(k, i, t):
        at = PAD + 8 * t
        part = pl.ds(8 * t, 8)
        field = v[k]
        x = field[i, pl.ds(at, 8), :]
        w = face_row[i - 1, part, :] * field[i - 1, pl.ds(at, 8), :]
        w += face_row[i, part, :] * field[i + 1, pl.ds(at, 8), :]
        w += face_left[i - 1, part, :] * field[i, pl.ds(at - 1, 8), :]
        w += face_right[i - 1, part, :] * field[i, pl.ds(at + 1, 8), :]
        w += face_down[i - 1, part, :] * pltpu.roll(x, 1, 1)
        w += face_up[i - 1, part, :] * pltpu.roll(x, depth - 1, 1)
        y = w * inv[i - 1, part, :]
        v[k + 1][i, pl.ds(at, 8), :] = y
        return w, x, y

    zero = jnp.zeros((8, 128), jnp.float32)
    lane128 = lax.broadcasted_iota(jnp.int32, (8, 128), 1)

    def part_copy(which, offset):
        return pltpu.make_async_remote_copy(
            src_ref=part_out.at[which],
            dst_ref=part_in.at[which, offset],
            send_sem=part_send.at[which, offset],
            recv_sem=part_recv.at[which, offset],
            device_id=peer(offset),
            device_id_type=MESH,
        )

    def send_parts(which, sums):
        tile = zero
        for d, s in enumerate(sums):
            tile = jnp.where(lane128 == d, jnp.sum(s, axis=(0, 1), keepdims=True), tile)
        part_out[which] = tile

        def one(offset, carry):
            part_copy(which, offset).start()
            return carry

        lax.fori_loop(1, n, one, 0)

    def take_parts(which, count):
        part_in[which, 0] = part_out[which]

        def wait(offset, carry):
            part_copy(which, offset).wait_recv()
            return carry

        lax.fori_loop(1, n, wait, 0)

        def add(p, tile):
            return tile + part_in[which, lax.rem(me - p + n, n)]

        tile = lax.fori_loop(0, n, add, zero)
        return [
            jnp.broadcast_to(
                jnp.sum(jnp.where(lane128 == d, tile, 0.0), axis=1, keepdims=True), (8, 128)
            )
            for d in range(count)
        ]

    def tiles_of(c):
        return range(c * width // 8, (c + 1) * width // 8)

    ends = ((0, 1), (1, rows))

    for a in (0, 1):
        for g in (0, 1):
            load(a, g).wait()
    for end, i in ends:
        for t in range(tiles):
            conduct(i, t)
    pl.semaphore_wait(barrier, n - 1)
    for c in range(cuts):
        for end, i in ends:
            send_row(0, end, c)
    send_edge(0, 0)
    load(0, 2).wait()
    load(1, 2).wait()

    def conduct_row(i, carry):
        for t in range(tiles):
            conduct(i, t)
        return carry

    lax.fori_loop(2, rows, conduct_row, 0)
    send_edge(0, 1)

    for a in (2, 3):
        for g in (0, 1):
            load(a, g).wait()
    wait_edge(0, 0)
    sums = [zero]
    for c in range(cuts):
        for end, i in ends:
            wait_row(0, end, c)
            for t in tiles_of(c):
                sums[0] = sums[0] + start_row(i, t, end)
            send_row(1, end, c)
    send_edge(1, 0)
    load(2, 2).wait()
    load(3, 2).wait()
    wait_edge(0, 1)

    def start_rows(i, acc):
        for t in range(tiles):
            acc = acc + start_row(i, t, None)
        return acc

    sums[0] = lax.fori_loop(2, rows, start_rows, sums[0])
    send_edge(1, 1)

    theta = bend = shift = gain = None
    for k in range(STEPS):
        last = k == STEPS - 1

        def visit(i, t, acc, k=k):
            w, x, y = apply(k, i, t)
            if k < 2:
                return (acc[0] + fold(w * x), acc[1] + fold(w * y))
            return acc

        acc = (zero, zero)
        wait_edge(k + 1, 0)
        for c in range(cuts):
            for end, i in ends:
                wait_row(k + 1, end, c)
                for t in tiles_of(c):
                    acc = visit(i, t, acc)
                if not last:
                    send_row(k + 2, end, c)
        if not last:
            send_edge(k + 2, 0)
        wait_edge(k + 1, 1)

        def visit_row(i, acc, visit=visit):
            for t in range(tiles):
                acc = visit(i, t, acc)
            return acc

        acc = lax.fori_loop(2, rows, visit_row, acc)
        if not last:
            send_edge(k + 2, 1)
        if k < 2:
            sums += list(acc)
        if k == 1:
            send_parts(0, sums)
        if k == 2:
            m = take_parts(0, 5)
            theta = m[1] / m[0]
            size = m[2] - theta * m[1]
            gain = jnp.maximum(size / m[0], 0.0)
            turn = m[3] - 2.0 * theta * m[2] + theta * theta * m[1]
            shift = jnp.where(size > 0.0, turn / jnp.where(size > 0.0, size, 1.0), 0.0)
            shift = jnp.minimum(jnp.maximum(shift, -1.0), 1.0)
            bend = shift * theta - gain
            slope = -(shift + theta)

    wide = lambda x: x[:, 0:1] * jnp.ones((1, depth), jnp.float32)
    theta_w, slope_w, bend_w = wide(theta), wide(slope), wide(bend)
    pairs = [(a, b) for a in range(4) for b in range(a, 5)]

    def gram_row(i, acc):
        acc = list(acc)
        for t in range(tiles):
            at = pl.ds(PAD + 8 * t, 8)
            f = [u[i, at, :] for u in v]
            d = diag[i - 1, pl.ds(8 * t, 8), :]
            q = [
                f[0],
                f[1] - theta_w * f[0],
                f[2] + slope_w * f[1] + bend_w * f[0],
                f[3] + slope_w * f[2] + bend_w * f[1],
                f[4] + slope_w * f[3] + bend_w * f[2],
            ]
            for a in range(4):
                dq = d * q[a]
                for b in range(a, 5):
                    spot = pairs.index((a, b))
                    acc[spot] = acc[spot] + fold(dq * q[b])
        return tuple(acc)

    grams = lax.fori_loop(1, rows + 1, gram_row, (zero,) * len(pairs))
    send_parts(1, grams)
    m = take_parts(1, len(pairs))
    gram = {}
    for (a, b), value in zip(pairs, m):
        gram[a, b] = gram[b, a] = value

    def times(p):
        out = [None] * 5
        def put(j, x):
            out[j] = x if out[j] is None else out[j] + x
        if p[0] is not None:
            put(0, theta * p[0])
            put(1, p[0])
        if p[1] is not None:
            put(0, gain * p[1])
            put(1, shift * p[1])
            put(2, p[1])
        if p[2] is not None:
            put(3, p[2])
        if p[3] is not None:
            put(4, p[3])
        return out

    def add(a, b, scale):
        out = []
        for x, y in zip(a, b):
            if y is None:
                out.append(x)
            elif x is None:
                out.append(scale * y)
            else:
                out.append(x + scale * y)
        return out

    def inner(a, b):
        total = None
        for i, x in enumerate(a):
            if x is None:
                continue
            line = None
            for j, y in enumerate(b):
                if y is not None:
                    term = gram[i, j] * y
                    line = term if line is None else line + term
            total = x * line if total is None else total + x * line
        return total

    one = jnp.ones((8, 128), jnp.float32)
    adj, res, way = [None] * 5, [one] + [None] * 4, [one] + [None] * 4
    norm = gram[0, 0]
    for step in range(STEPS):
        image = add(way, times(way), -one)
        alpha = norm / inner(way, image)
        adj = add(adj, way, alpha)
        res = add(res, image, -alpha)
        if step + 1 < STEPS:
            after = inner(res, res)
            way = add(res, way, after / norm)
            norm = after

    def back(q):
        q = [zero if x is None else x for x in q]
        return [
            q[0] - theta * q[1] + bend * q[2],
            q[1] + slope * q[2] + bend * q[3],
            q[2] + slope * q[3] + bend * q[4],
            q[3] + slope * q[4],
            q[4],
        ]

    adj_w = [wide(x) for x in back(adj)[:4]]
    res_w = [wide(x) for x in back(res)]

    def finish_row(i, carry):
        for t in range(tiles):
            at = pl.ds(PAD + 8 * t, 8)
            part = pl.ds(8 * t, 8)
            f = [u[i, at, :] for u in v]
            x = adj_w[0] * f[0]
            for j in range(1, 4):
                x += adj_w[j] * f[j]
            r = res_w[0] * f[0]
            for j in range(1, 5):
                r += res_w[j] * f[j]
            adjoint_ref[i - 1, part, :] = x
            residual_ref[i - 1, part, :] = r * diag[i - 1, part, :]
        return carry

    lax.fori_loop(1, rows + 1, finish_row, 0)

    for k in range(STEPS + 1):
        for group in (0, 1):
            edge_copy(k, group).wait_send()
        for side in (0, 1):
            @pl.when(has(side))
            def _(k=k, side=side):
                for c in range(cuts):
                    row_copy(k, side, c).wait_send()

    def sent(offset, carry):
        for which in (0, 1):
            part_copy(which, offset).wait_send()
        return carry

    lax.fori_loop(1, n, sent, 0)


def per_device(ngx, ngy, cuts, temp, label, flag, source, k0, tc, ts):
    rows, cols, depth = temp.shape
    n = ngx * ngy
    block = lambda dtype: pltpu.VMEM((rows, cols, depth), dtype)
    padded = pltpu.VMEM((rows + 2, cols + 2 * PAD, depth), jnp.float32)
    f32 = jnp.float32
    out = jax.ShapeDtypeStruct((rows, cols, depth), f32)
    dma = pltpu.SemaphoreType.DMA
    return pl.pallas_call(
        functools.partial(kernel, ngx, ngy, cuts),
        out_shape=(out, out),
        in_specs=[pl.BlockSpec(memory_space=pl.ANY)] * 4
        + [pl.BlockSpec(memory_space=pltpu.SMEM)] * 3,
        out_specs=(pl.BlockSpec(memory_space=pltpu.VMEM),) * 2,
        scratch_shapes=[block(f32), block(jnp.int32), block(jnp.int32), block(f32)]
        + [padded] * 6
        + [pltpu.VMEM((rows + 1, cols, depth), f32)]
        + [block(f32)] * 6
        + [
            pltpu.VMEM((STEPS + 1, 16, depth), f32),
            pltpu.VMEM((STEPS + 1, 16, depth), f32),
            pltpu.VMEM((2, 8, 128), f32),
            pltpu.VMEM((2, n, 8, 128), f32),
            dma((4, 3)),
            dma((STEPS + 1, 2, cuts)),
            dma((STEPS + 1, 2, cuts)),
            dma((STEPS + 1, 2)),
            dma((STEPS + 1, 2)),
            dma((2, n)),
            dma((2, n)),
        ],
        compiler_params=pltpu.CompilerParams(
            collective_id=0, has_side_effects=True, vmem_limit_bytes=48 * 1024 * 1024
        ),
    )(temp, label, flag, source, k0, tc, ts)


def solution(mesh):
    block = P(("cycle", "gx"), "gy", None)
    shared = P("gx", "gy", None)
    return jax.shard_map(
        functools.partial(per_device, mesh.shape["gx"], mesh.shape["gy"], 2),
        mesh=mesh,
        in_specs=(block, shared, shared, block, P(), P(), P()),
        out_specs=(block, block),
        check_vma=False,
    )
```

```python
import functools

import jax
import jax.numpy as jnp
from jax import lax
from jax.experimental import pallas as pl
from jax.experimental.pallas import tpu as pltpu
from jax.sharding import PartitionSpec as P

HCOOL = 1.5
STEPS = 4
PAD = 8
MESH = pl.DeviceIdType.MESH


def fold(x):
    total = x[:, :128]
    for lane in range(128, x.shape[1], 128):
        total = total + x[:, lane : lane + 128]
    return total


def harmonic(a, b):
    return 2.0 * a * b / (a + b)


def spread(x):
    return jnp.broadcast_to(jnp.sum(x, axis=(0, 1), keepdims=True), (8, 128))


def kernel(
    ngx, ngy, cuts,
    temp_hbm, label_hbm, flag_hbm, source_hbm, k0_hbm, tc_hbm, ts_hbm,
    adjoint_ref, residual_ref,
    k0_ref, tc_ref, ts_ref, temp, label, flag, source, fields,
    scalars, sums, face_row, face_left, face_right, face_down, face_up, inv, diag,
    edge_out, edge_in, part_out, part_in,
    load_sem, table_sem, row_send, row_recv, edge_send, edge_recv, part_send, part_recv,
):
    rows, cols, depth = temp.shape
    tiles = cols // 8
    gx, gy = lax.axis_index("gx"), lax.axis_index("gy")
    n = ngx * ngy
    me = gx * ngy + gy
    cond, v0 = fields.at[0], fields.at[1]
    has_lower, has_upper = gx > 0, gx < ngx - 1

    def peer(offset):
        p = lax.rem(me + offset, n)
        return {"gx": p // ngy, "gy": lax.rem(p, ngy)}

    def load(a, group):
        src, dst = ((temp_hbm, temp), (label_hbm, label), (source_hbm, source), (flag_hbm, flag))[a]
        first, size = ((0, 1), (rows - 1, 1), (1, rows - 2))[group]
        return pltpu.make_async_copy(
            src.at[pl.ds(first, size)], dst.at[pl.ds(first, size)], load_sem.at[a, group]
        )

    tables = [
        pltpu.make_async_copy(src, dst, table_sem.at[j])
        for j, (src, dst) in enumerate(((k0_hbm, k0_ref), (tc_hbm, tc_ref), (ts_hbm, ts_ref)))
    ]
    for copy in tables:
        copy.start()
    order = [(a, g) for a in (0, 1) for g in (0, 1)] + [(a, g) for a in (2, 3) for g in (0, 1)]
    order += [(a, 2) for a in range(4)]
    for a, g in order:
        load(a, g).start()

    barrier = pltpu.get_barrier_semaphore()

    def greet(offset, carry):
        pl.semaphore_signal(barrier, inc=1, device_id=peer(offset), device_id_type=MESH)
        return carry

    lax.fori_loop(1, n, greet, 0)

    zero_row = jnp.zeros((cols, depth), jnp.float32)
    zero_edge = jnp.zeros((8, depth), jnp.float32)

    def clear(k, carry):
        @pl.when(jnp.logical_not(has_lower))
        def _():
            fields[k, 0, PAD : PAD + cols, :] = zero_row

        @pl.when(jnp.logical_not(has_upper))
        def _():
            fields[k, rows + 1, PAD : PAD + cols, :] = zero_row

        def clear_edge(i, carry):
            fields[k, i, 0:PAD, :] = zero_edge
            fields[k, i, PAD + cols : PAD + cols + 8, :] = zero_edge
            return carry

        lax.fori_loop(1, rows + 1, clear_edge, 0)
        edge_out[k, 0:8, :] = zero_edge
        edge_out[k, 8:16, :] = zero_edge
        return carry

    lax.fori_loop(0, STEPS + 1, clear, 0)

    width = cols // cuts
    own_edge = jnp.where(gy == 0, PAD + cols - 1, PAD)
    halo_edge = jnp.where(gy == 0, PAD + cols, PAD - 1)

    def row_copy(k, side, c):
        src = 1 + side * (rows - 1)
        dst = (1 - side) * (rows + 1)
        part = pl.ds(PAD + c * width, width)
        return pltpu.make_async_remote_copy(
            src_ref=fields.at[k, src, part, :],
            dst_ref=fields.at[k, dst, part, :],
            send_sem=row_send.at[k, side, c],
            recv_sem=row_recv.at[k, side, c],
            device_id={"gx": gx - 1 + 2 * side},
            device_id_type=MESH,
        )

    def has(side):
        return jnp.where(side == 0, gx, ngx - 1 - gx) > 0

    def send_row(k, side, c):
        @pl.when(has(side))
        def _():
            row_copy(k, side, c).start()

    def wait_row(k, end, c):
        @pl.when(has(end))
        def _():
            row_copy(k, 1 - end, c).wait_recv()

    def edge_copy(k, group):
        part = pl.ds(8 * group, 8)
        return pltpu.make_async_remote_copy(
            src_ref=edge_out.at[k, part, :],
            dst_ref=edge_in.at[k, part, :],
            send_sem=edge_send.at[k, group],
            recv_sem=edge_recv.at[k, group],
            device_id={"gy": 1 - gy},
            device_id_type=MESH,
        )

    def outer(j):
        return 1 + j * (rows - 1), j

    def others(j):
        return j + 2, j + 8

    groups = ((2, outer), (rows - 2, others))

    def send_edge(k, group):
        count, spot_of = groups[group]

        def one(j, carry):
            i, spot = spot_of(j)
            edge_out[k, pl.ds(spot, 1), :] = fields[k, i, pl.ds(own_edge, 1), :]
            return carry

        lax.fori_loop(0, count, one, 0)
        edge_copy(k, group).start()

    def wait_edge(k, group):
        edge_copy(k, group).wait_recv()
        count, spot_of = groups[group]

        def one(j, carry):
            i, spot = spot_of(j)
            fields[k, i, pl.ds(halo_edge, 1), :] = edge_in[k, pl.ds(spot, 1), :]
            return carry

        lax.fori_loop(0, count, one, 0)

    def table(ref, marks):
        out = jnp.zeros(marks[0].shape, jnp.float32)
        for m, mark in enumerate(marks):
            out = jnp.where(mark, ref[m], out)
        return out

    def conduct(i, t):
        part = pl.ds(8 * t, 8)
        kind = label[i - 1, part, :]
        marks = [kind == m for m in range(k0_ref.shape[0])]
        cond[i, pl.ds(PAD + 8 * t, 8), :] = table(k0_ref, marks) * (
            1.0 + table(tc_ref, marks) * temp[i - 1, part, :]
        )

    def start_row(i, t):
        at = PAD + 8 * t
        part = pl.ds(8 * t, 8)
        c = cond[i, pl.ds(at, 8), :]
        lower = harmonic(c, cond[i - 1, pl.ds(at, 8), :])
        upper = harmonic(c, cond[i + 1, pl.ds(at, 8), :])
        left = harmonic(c, cond[i, pl.ds(at - 1, 8), :])
        right = harmonic(c, cond[i, pl.ds(at + 1, 8), :])
        lane = lax.broadcasted_iota(jnp.int32, c.shape, 1)
        down = harmonic(c, jnp.where(lane == 0, 0.0, pltpu.roll(c, 1, 1)))
        up = pltpu.roll(down, depth - 1, 1)
        face_row[i - 1, part, :] = lower
        face_row[i, part, :] = upper
        face_left[i - 1, part, :] = left
        face_right[i - 1, part, :] = right
        face_down[i - 1, part, :] = down
        face_up[i - 1, part, :] = up
        kind = label[i - 1, part, :]
        marks = [kind == m for m in range(k0_ref.shape[0])]
        base = table(ts_ref, marks) + HCOOL * flag[i - 1, part, :].astype(jnp.float32)
        d = base + lower + upper + left + right + down + up
        s = source[i - 1, part, :]
        over = 1.0 / d
        diag[i - 1, part, :] = d
        inv[i - 1, part, :] = over
        z = s * over
        v0[i, pl.ds(at, 8), :] = z
        return fold(z * s)

    def apply(k, i, t):
        at = PAD + 8 * t
        part = pl.ds(8 * t, 8)
        field = fields.at[k + 1]
        x = field[i, pl.ds(at, 8), :]
        w = face_row[i - 1, part, :] * field[i - 1, pl.ds(at, 8), :]
        w += face_row[i, part, :] * field[i + 1, pl.ds(at, 8), :]
        w += face_left[i - 1, part, :] * field[i, pl.ds(at - 1, 8), :]
        w += face_right[i - 1, part, :] * field[i, pl.ds(at + 1, 8), :]
        w += face_down[i - 1, part, :] * pltpu.roll(x, 1, 1)
        w += face_up[i - 1, part, :] * pltpu.roll(x, depth - 1, 1)
        y = w * inv[i - 1, part, :]
        fields[k + 2, i, pl.ds(at, 8), :] = y
        return w, x, y

    zero = jnp.zeros((8, 128), jnp.float32)
    lane128 = lax.broadcasted_iota(jnp.int32, (8, 128), 1)

    def part_copy(which, offset):
        return pltpu.make_async_remote_copy(
            src_ref=part_out.at[which],
            dst_ref=part_in.at[which, offset],
            send_sem=part_send.at[which, offset],
            recv_sem=part_recv.at[which, offset],
            device_id=peer(offset),
            device_id_type=MESH,
        )

    def send_parts(which, terms):
        tile = zero
        for d, s in enumerate(terms):
            tile = jnp.where(lane128 == d, jnp.sum(s, axis=(0, 1), keepdims=True), tile)
        part_out[which] = tile

        def one(offset, carry):
            part_copy(which, offset).start()
            return carry

        lax.fori_loop(1, n, one, 0)

    def take_parts(which, count):
        part_in[which, 0] = part_out[which]

        def wait(offset, carry):
            part_copy(which, offset).wait_recv()
            return carry

        lax.fori_loop(1, n, wait, 0)

        def add(p, tile):
            return tile + part_in[which, lax.rem(me - p + n, n)]

        tile = lax.fori_loop(0, n, add, zero)
        return [
            jnp.broadcast_to(
                jnp.sum(jnp.where(lane128 == d, tile, 0.0), axis=1, keepdims=True), (8, 128)
            )
            for d in range(count)
        ]

    def tiles_of(c):
        return range(c * width // 8, (c + 1) * width // 8)

    def each_end(visit, carry):
        def one(end, carry):
            return visit(end, 1 + end * (rows - 1), carry)

        return lax.fori_loop(0, 2, one, carry)

    for copy in tables:
        copy.wait()
    for a in (0, 1):
        for g in (0, 1):
            load(a, g).wait()

    def conduct_row(i, carry):
        for t in range(tiles):
            conduct(i, t)
        return carry

    each_end(lambda end, i, carry: conduct_row(i, carry), 0)
    pl.semaphore_wait(barrier, n - 1)
    for c in range(cuts):
        for end in (0, 1):
            send_row(0, end, c)
    send_edge(0, 0)
    load(0, 2).wait()
    load(1, 2).wait()
    lax.fori_loop(2, rows, conduct_row, 0)
    send_edge(0, 1)

    for a in (2, 3):
        for g in (0, 1):
            load(a, g).wait()
    wait_edge(0, 0)
    acc = zero
    for c in range(cuts):

        def start_end(end, i, acc, c=c):
            wait_row(0, end, c)
            for t in tiles_of(c):
                acc = acc + start_row(i, t)
            send_row(1, end, c)
            return acc

        acc = each_end(start_end, acc)
    send_edge(1, 0)
    load(2, 2).wait()
    load(3, 2).wait()
    wait_edge(0, 1)

    def start_rows(i, acc):
        for t in range(tiles):
            acc = acc + start_row(i, t)
        return acc

    sums[0] = lax.fori_loop(2, rows, start_rows, acc)
    send_edge(1, 1)

    def step(k, carry):
        more = k < STEPS - 1

        def visit(i, t, acc):
            w, x, y = apply(k, i, t)
            if k >= 2:
                return acc
            return (acc[0] + fold(w * x), acc[1] + fold(w * y))

        acc = (zero, zero)
        wait_edge(k + 1, 0)
        for c in range(cuts):

            def visit_end(end, i, acc, c=c):
                wait_row(k + 1, end, c)
                for t in tiles_of(c):
                    acc = visit(i, t, acc)

                @pl.when(more)
                def _():
                    send_row(k + 2, end, c)

                return acc

            acc = each_end(visit_end, acc)

        @pl.when(more)
        def _():
            send_edge(k + 2, 0)

        wait_edge(k + 1, 1)

        def visit_row(i, acc):
            for t in range(tiles):
                acc = visit(i, t, acc)
            return acc

        acc = lax.fori_loop(2, rows, visit_row, acc)

        @pl.when(more)
        def _():
            send_edge(k + 2, 1)

        if k < 2:
            sums[2 * k + 1] = acc[0]
            sums[2 * k + 2] = acc[1]

        @pl.when(k == 1)
        def _():
            send_parts(0, [sums[j] for j in range(5)])

        @pl.when(k == 2)
        def _():
            m = take_parts(0, 5)
            theta = m[1] / m[0]
            size = m[2] - theta * m[1]
            gain = jnp.maximum(size / m[0], 0.0)
            turn = m[3] - 2.0 * theta * m[2] + theta * theta * m[1]
            shift = jnp.where(size > 0.0, turn / jnp.where(size > 0.0, size, 1.0), 0.0)
            shift = jnp.minimum(jnp.maximum(shift, -1.0), 1.0)
            scalars[0] = theta
            scalars[1] = shift
            scalars[2] = gain

        return carry

    for k in range(STEPS):
        step(k, 0)
    theta, shift, gain = scalars[0], scalars[1], scalars[2]
    slope = -(shift + theta)
    bend = shift * theta - gain

    wide = lambda x: x[:, 0:1] * jnp.ones((1, depth), jnp.float32)
    theta_w, slope_w, bend_w = wide(theta), wide(slope), wide(bend)
    pairs = [(a, b) for a in range(4) for b in range(a, 5)]

    def gram_row(i, acc):
        acc = list(acc)
        for t in range(tiles):
            at = pl.ds(PAD + 8 * t, 8)
            f = [fields[j, i, at, :] for j in range(1, STEPS + 2)]
            d = diag[i - 1, pl.ds(8 * t, 8), :]
            q = [
                f[0],
                f[1] - theta_w * f[0],
                f[2] + slope_w * f[1] + bend_w * f[0],
                f[3] + slope_w * f[2] + bend_w * f[1],
                f[4] + slope_w * f[3] + bend_w * f[2],
            ]
            for a in range(4):
                dq = d * q[a]
                for b in range(a, 5):
                    spot = pairs.index((a, b))
                    acc[spot] = acc[spot] + fold(dq * q[b])
        return tuple(acc)

    grams = lax.fori_loop(1, rows + 1, gram_row, (zero,) * len(pairs))
    send_parts(1, grams)
    m = take_parts(1, len(pairs))
    gram = {}
    for (a, b), value in zip(pairs, m):
        gram[a, b] = gram[b, a] = value

    def times(p):
        out = [None] * 5
        def put(j, x):
            out[j] = x if out[j] is None else out[j] + x
        if p[0] is not None:
            put(0, theta * p[0])
            put(1, p[0])
        if p[1] is not None:
            put(0, gain * p[1])
            put(1, shift * p[1])
            put(2, p[1])
        if p[2] is not None:
            put(3, p[2])
        if p[3] is not None:
            put(4, p[3])
        return out

    def add(a, b, scale):
        out = []
        for x, y in zip(a, b):
            if y is None:
                out.append(x)
            elif x is None:
                out.append(scale * y)
            else:
                out.append(x + scale * y)
        return out

    def inner(a, b):
        total = None
        for i, x in enumerate(a):
            if x is None:
                continue
            line = None
            for j, y in enumerate(b):
                if y is not None:
                    term = gram[i, j] * y
                    line = term if line is None else line + term
            total = x * line if total is None else total + x * line
        return total

    one = jnp.ones((8, 128), jnp.float32)
    adj, res, way = [None] * 5, [one] + [None] * 4, [one] + [None] * 4
    norm = gram[0, 0]
    for step in range(STEPS):
        image = add(way, times(way), -one)
        alpha = norm / inner(way, image)
        adj = add(adj, way, alpha)
        res = add(res, image, -alpha)
        if step + 1 < STEPS:
            after = inner(res, res)
            way = add(res, way, after / norm)
            norm = after

    def back(q):
        q = [zero if x is None else x for x in q]
        return [
            q[0] - theta * q[1] + bend * q[2],
            q[1] + slope * q[2] + bend * q[3],
            q[2] + slope * q[3] + bend * q[4],
            q[3] + slope * q[4],
            q[4],
        ]

    adj_w = [wide(x) for x in back(adj)[:4]]
    res_w = [wide(x) for x in back(res)]

    def finish_row(i, carry):
        for t in range(tiles):
            at = pl.ds(PAD + 8 * t, 8)
            part = pl.ds(8 * t, 8)
            f = [fields[j, i, at, :] for j in range(1, STEPS + 2)]
            x = adj_w[0] * f[0]
            for j in range(1, 4):
                x += adj_w[j] * f[j]
            r = res_w[0] * f[0]
            for j in range(1, 5):
                r += res_w[j] * f[j]
            adjoint_ref[i - 1, part, :] = x
            residual_ref[i - 1, part, :] = r * diag[i - 1, part, :]
        return carry

    lax.fori_loop(1, rows + 1, finish_row, 0)

    def left(k, carry):
        for group in (0, 1):
            edge_copy(k, group).wait_send()

        def one(side, carry):
            @pl.when(has(side))
            def _():
                for c in range(cuts):
                    row_copy(k, side, c).wait_send()

            return carry

        return lax.fori_loop(0, 2, one, carry)

    lax.fori_loop(0, STEPS + 1, left, 0)

    def sent(offset, carry):
        for which in (0, 1):
            part_copy(which, offset).wait_send()
        return carry

    lax.fori_loop(1, n, sent, 0)


def per_device(ngx, ngy, cuts, temp, label, flag, source, k0, tc, ts):
    rows, cols, depth = temp.shape
    n = ngx * ngy
    block = lambda dtype: pltpu.VMEM((rows, cols, depth), dtype)
    padded = pltpu.VMEM((STEPS + 2, rows + 2, cols + 2 * PAD, depth), jnp.float32)
    f32 = jnp.float32
    out = jax.ShapeDtypeStruct((rows, cols, depth), f32)
    dma = pltpu.SemaphoreType.DMA
    return pl.pallas_call(
        functools.partial(kernel, ngx, ngy, cuts),
        out_shape=(out, out),
        in_specs=[pl.BlockSpec(memory_space=pltpu.HBM)] * 7,
        out_specs=(pl.BlockSpec(memory_space=pltpu.VMEM),) * 2,
        scratch_shapes=[pltpu.SMEM(k0.shape, f32)] * 3
        + [block(f32), block(jnp.int32), block(jnp.int32), block(f32)]
        + [padded, pltpu.VMEM((3, 8, 128), f32), pltpu.VMEM((5, 8, 128), f32)]
        + [pltpu.VMEM((rows + 1, cols, depth), f32)]
        + [block(f32)] * 6
        + [
            pltpu.VMEM((STEPS + 1, 16, depth), f32),
            pltpu.VMEM((STEPS + 1, 16, depth), f32),
            pltpu.VMEM((2, 8, 128), f32),
            pltpu.VMEM((2, n, 8, 128), f32),
            dma((4, 3)),
            dma((3,)),
            dma((STEPS + 1, 2, cuts)),
            dma((STEPS + 1, 2, cuts)),
            dma((STEPS + 1, 2)),
            dma((STEPS + 1, 2)),
            dma((2, n)),
            dma((2, n)),
        ],
        compiler_params=pltpu.CompilerParams(
            collective_id=0, has_side_effects=True, vmem_limit_bytes=62 * 1024 * 1024
        ),
    )(temp, label, flag, source, k0, tc, ts)


def solution(mesh):
    block = P(("cycle", "gx"), "gy", None)
    shared = P("gx", "gy", None)
    return jax.shard_map(
        functools.partial(per_device, mesh.shape["gx"], mesh.shape["gy"], 4),
        mesh=mesh,
        in_specs=(block, shared, shared, block, P(), P(), P()),
        out_specs=(block, block),
        check_vma=False,
    )
```

```python
import functools

import jax
import jax.numpy as jnp
from jax import lax
from jax.experimental import pallas as pl
from jax.experimental.pallas import tpu as pltpu
from jax.sharding import PartitionSpec as P

HCOOL = 1.5
STEPS = 4
PAD = 8
MESH = pl.DeviceIdType.MESH


def fold(x):
    total = x[:, :128]
    for lane in range(128, x.shape[1], 128):
        total = total + x[:, lane : lane + 128]
    return total


def harmonic(a, b):
    return 2.0 * a * b / (a + b)


def spread(x):
    return jnp.broadcast_to(jnp.sum(x, axis=(0, 1), keepdims=True), (8, 128))


def kernel(
    ngx, ngy, cuts,
    temp_hbm, label_hbm, flag_hbm, source_hbm, k0_hbm, tc_hbm, ts_hbm,
    adjoint_ref, residual_ref,
    k0_ref, tc_ref, ts_ref, temp, label, flag, source, fields,
    scalars, sums, face_row, face_left, face_right, face_down, face_up, inv, diag,
    edge_out, edge_in, part_out, part_in,
    load_sem, table_sem, row_send, row_recv, edge_send, edge_recv, part_send, part_recv,
):
    rows, cols, depth = temp.shape
    tiles = cols // 8
    gx, gy = lax.axis_index("gx"), lax.axis_index("gy")
    n = ngx * ngy
    me = gx * ngy + gy
    cond, v0 = fields.at[0], fields.at[1]
    has_lower, has_upper = gx > 0, gx < ngx - 1

    def peer(offset):
        p = lax.rem(me + offset, n)
        return {"gx": p // ngy, "gy": lax.rem(p, ngy)}

    def load(a, group):
        src, dst = ((temp_hbm, temp), (label_hbm, label), (source_hbm, source), (flag_hbm, flag))[a]
        first, size = ((0, 1), (rows - 1, 1), (1, rows - 2))[group]
        return pltpu.make_async_copy(
            src.at[pl.ds(first, size)], dst.at[pl.ds(first, size)], load_sem.at[a, group]
        )

    tables = [
        pltpu.make_async_copy(src, dst, table_sem.at[j])
        for j, (src, dst) in enumerate(((k0_hbm, k0_ref), (tc_hbm, tc_ref), (ts_hbm, ts_ref)))
    ]
    for copy in tables:
        copy.start()
    order = [(a, g) for a in (0, 1) for g in (0, 1)] + [(a, g) for a in (2, 3) for g in (0, 1)]
    order += [(a, 2) for a in range(4)]
    for a, g in order:
        load(a, g).start()

    barrier = pltpu.get_barrier_semaphore()

    def greet(offset, carry):
        pl.semaphore_signal(barrier, inc=1, device_id=peer(offset), device_id_type=MESH)
        return carry

    lax.fori_loop(1, n, greet, 0)

    zero_row = jnp.zeros((cols, depth), jnp.float32)
    zero_edge = jnp.zeros((8, depth), jnp.float32)

    def clear(k, carry):
        @pl.when(jnp.logical_not(has_lower))
        def _():
            fields[k, 0, PAD : PAD + cols, :] = zero_row

        @pl.when(jnp.logical_not(has_upper))
        def _():
            fields[k, rows + 1, PAD : PAD + cols, :] = zero_row

        def clear_edge(i, carry):
            fields[k, i, 0:PAD, :] = zero_edge
            fields[k, i, PAD + cols : PAD + cols + 8, :] = zero_edge
            return carry

        lax.fori_loop(1, rows + 1, clear_edge, 0)
        edge_out[k, 0:8, :] = zero_edge
        edge_out[k, 8:16, :] = zero_edge
        return carry

    lax.fori_loop(0, STEPS + 1, clear, 0)

    width = cols // cuts
    own_edge = jnp.where(gy == 0, PAD + cols - 1, PAD)
    halo_edge = jnp.where(gy == 0, PAD + cols, PAD - 1)

    def row_copy(k, side, c):
        src = 1 + side * (rows - 1)
        dst = (1 - side) * (rows + 1)
        part = pl.ds(PAD + c * width, width)
        return pltpu.make_async_remote_copy(
            src_ref=fields.at[k, src, part, :],
            dst_ref=fields.at[k, dst, part, :],
            send_sem=row_send.at[k, side, c],
            recv_sem=row_recv.at[k, side, c],
            device_id={"gx": gx - 1 + 2 * side},
            device_id_type=MESH,
        )

    def has(side):
        return jnp.where(side == 0, gx, ngx - 1 - gx) > 0

    def send_row(k, side, c):
        @pl.when(has(side))
        def _():
            row_copy(k, side, c).start()

    def wait_row(k, end, c):
        @pl.when(has(end))
        def _():
            row_copy(k, 1 - end, c).wait_recv()

    def edge_copy(k, group):
        part = pl.ds(8 * group, 8)
        return pltpu.make_async_remote_copy(
            src_ref=edge_out.at[k, part, :],
            dst_ref=edge_in.at[k, part, :],
            send_sem=edge_send.at[k, group],
            recv_sem=edge_recv.at[k, group],
            device_id={"gy": 1 - gy},
            device_id_type=MESH,
        )

    def outer(j):
        return 1 + j * (rows - 1), j

    def others(j):
        return j + 2, j + 8

    groups = ((2, outer), (rows - 2, others))

    def send_edge(k, group):
        count, spot_of = groups[group]

        def one(j, carry):
            i, spot = spot_of(j)
            edge_out[k, pl.ds(spot, 1), :] = fields[k, i, pl.ds(own_edge, 1), :]
            return carry

        lax.fori_loop(0, count, one, 0)
        edge_copy(k, group).start()

    def wait_edge(k, group):
        edge_copy(k, group).wait_recv()
        count, spot_of = groups[group]

        def one(j, carry):
            i, spot = spot_of(j)
            fields[k, i, pl.ds(halo_edge, 1), :] = edge_in[k, pl.ds(spot, 1), :]
            return carry

        lax.fori_loop(0, count, one, 0)

    def table(ref, marks):
        out = jnp.zeros(marks[0].shape, jnp.float32)
        for m, mark in enumerate(marks):
            out = jnp.where(mark, ref[m], out)
        return out

    def conduct(i, t):
        part = pl.ds(8 * t, 8)
        kind = label[i - 1, part, :]
        marks = [kind == m for m in range(k0_ref.shape[0])]
        cond[i, pl.ds(PAD + 8 * t, 8), :] = table(k0_ref, marks) * (
            1.0 + table(tc_ref, marks) * temp[i - 1, part, :]
        )

    def start_row(i, t):
        at = PAD + 8 * t
        part = pl.ds(8 * t, 8)
        c = cond[i, pl.ds(at, 8), :]
        lower = harmonic(c, cond[i - 1, pl.ds(at, 8), :])
        upper = harmonic(c, cond[i + 1, pl.ds(at, 8), :])
        left = harmonic(c, cond[i, pl.ds(at - 1, 8), :])
        right = harmonic(c, cond[i, pl.ds(at + 1, 8), :])
        lane = lax.broadcasted_iota(jnp.int32, c.shape, 1)
        down = harmonic(c, jnp.where(lane == 0, 0.0, pltpu.roll(c, 1, 1)))
        up = pltpu.roll(down, depth - 1, 1)
        face_row[i - 1, part, :] = lower
        face_row[i, part, :] = upper
        face_left[i - 1, part, :] = left
        face_right[i - 1, part, :] = right
        face_down[i - 1, part, :] = down
        face_up[i - 1, part, :] = up
        kind = label[i - 1, part, :]
        marks = [kind == m for m in range(k0_ref.shape[0])]
        base = table(ts_ref, marks) + HCOOL * flag[i - 1, part, :].astype(jnp.float32)
        d = base + lower + upper + left + right + down + up
        s = source[i - 1, part, :]
        over = 1.0 / d
        diag[i - 1, part, :] = d
        inv[i - 1, part, :] = over
        z = s * over
        v0[i, pl.ds(at, 8), :] = z
        return fold(z * s)

    def apply(k, i, t):
        at = PAD + 8 * t
        part = pl.ds(8 * t, 8)
        field = fields.at[k + 1]
        x = field[i, pl.ds(at, 8), :]
        w = face_row[i - 1, part, :] * field[i - 1, pl.ds(at, 8), :]
        w += face_row[i, part, :] * field[i + 1, pl.ds(at, 8), :]
        w += face_left[i - 1, part, :] * field[i, pl.ds(at - 1, 8), :]
        w += face_right[i - 1, part, :] * field[i, pl.ds(at + 1, 8), :]
        w += face_down[i - 1, part, :] * pltpu.roll(x, 1, 1)
        w += face_up[i - 1, part, :] * pltpu.roll(x, depth - 1, 1)
        y = w * inv[i - 1, part, :]
        fields[k + 2, i, pl.ds(at, 8), :] = y
        return w, x, y

    zero = jnp.zeros((8, 128), jnp.float32)
    lane128 = lax.broadcasted_iota(jnp.int32, (8, 128), 1)

    def part_copy(which, offset):
        return pltpu.make_async_remote_copy(
            src_ref=part_out.at[which],
            dst_ref=part_in.at[which, offset],
            send_sem=part_send.at[which, offset],
            recv_sem=part_recv.at[which, offset],
            device_id=peer(offset),
            device_id_type=MESH,
        )

    def send_parts(which, terms):
        tile = zero
        for d, s in enumerate(terms):
            tile = jnp.where(lane128 == d, jnp.sum(s, axis=(0, 1), keepdims=True), tile)
        part_out[which] = tile

        def one(offset, carry):
            part_copy(which, offset).start()
            return carry

        lax.fori_loop(1, n, one, 0)

    def take_parts(which, count):
        part_in[which, 0] = part_out[which]

        def wait(offset, carry):
            part_copy(which, offset).wait_recv()
            return carry

        lax.fori_loop(1, n, wait, 0)

        def add(p, tile):
            return tile + part_in[which, lax.rem(me - p + n, n)]

        tile = lax.fori_loop(0, n, add, zero)
        return [
            jnp.broadcast_to(
                jnp.sum(jnp.where(lane128 == d, tile, 0.0), axis=1, keepdims=True), (8, 128)
            )
            for d in range(count)
        ]

    def tiles_of(c):
        return range(c * width // 8, (c + 1) * width // 8)

    def each_end(visit, carry):
        def one(end, carry):
            return visit(end, 1 + end * (rows - 1), carry)

        return lax.fori_loop(0, 2, one, carry)

    for copy in tables:
        copy.wait()
    for a in (0, 1):
        for g in (0, 1):
            load(a, g).wait()

    def conduct_row(i, carry):
        for t in range(tiles):
            conduct(i, t)
        return carry

    each_end(lambda end, i, carry: conduct_row(i, carry), 0)
    pl.semaphore_wait(barrier, n - 1)
    for c in range(cuts):
        for end in (0, 1):
            send_row(0, end, c)
    send_edge(0, 0)
    load(0, 2).wait()
    load(1, 2).wait()
    lax.fori_loop(2, rows, conduct_row, 0)
    send_edge(0, 1)

    for a in (2, 3):
        for g in (0, 1):
            load(a, g).wait()
    wait_edge(0, 0)
    acc = zero
    for c in range(cuts):

        def start_end(end, i, acc, c=c):
            wait_row(0, end, c)
            for t in tiles_of(c):
                acc = acc + start_row(i, t)
            send_row(1, end, c)
            return acc

        acc = each_end(start_end, acc)
    send_edge(1, 0)
    load(2, 2).wait()
    load(3, 2).wait()
    wait_edge(0, 1)

    def start_rows(i, acc):
        for t in range(tiles):
            acc = acc + start_row(i, t)
        return acc

    sums[0] = lax.fori_loop(2, rows, start_rows, acc)
    send_edge(1, 1)

    wide = lambda x: x[:, 0:1] * jnp.ones((1, depth), jnp.float32)
    early = [(a, b) for a in range(4) for b in range(a, 4)]
    late = [(a, 4) for a in range(4)]
    pairs = early + late

    def gram_of(first):
        theta, shift, gain = scalars[0], scalars[1], scalars[2]
        theta_w = wide(theta)
        slope_w = wide(-(shift + theta))
        bend_w = wide(shift * theta - gain)
        here = early if first else late

        def gram_row(i, acc):
            acc = list(acc)
            for t in range(tiles):
                at = pl.ds(PAD + 8 * t, 8)
                f = [fields[j, i, at, :] for j in range(1, STEPS + (1 if first else 2))]
                d = diag[i - 1, pl.ds(8 * t, 8), :]
                q = [f[0], f[1] - theta_w * f[0]]
                for j in range(2, len(f)):
                    q.append(f[j] + slope_w * f[j - 1] + bend_w * f[j - 2])
                if first:
                    for a in range(4):
                        dq = d * q[a]
                        for b in range(a, 4):
                            spot = here.index((a, b))
                            acc[spot] = acc[spot] + fold(dq * q[b])
                else:
                    dq = d * q[4]
                    for a in range(4):
                        acc[a] = acc[a] + fold(dq * q[a])
            return tuple(acc)

        return lax.fori_loop(1, rows + 1, gram_row, (zero,) * len(here))

    def step(k, carry):
        more = k < STEPS - 1

        def visit(i, t, acc):
            w, x, y = apply(k, i, t)
            if k >= 2:
                return acc
            return (acc[0] + fold(w * x), acc[1] + fold(w * y))

        acc = (zero, zero)
        wait_edge(k + 1, 0)
        for c in range(cuts):

            def visit_end(end, i, acc, c=c):
                wait_row(k + 1, end, c)
                for t in tiles_of(c):
                    acc = visit(i, t, acc)

                @pl.when(more)
                def _():
                    send_row(k + 2, end, c)

                return acc

            acc = each_end(visit_end, acc)

        @pl.when(more)
        def _():
            send_edge(k + 2, 0)

        wait_edge(k + 1, 1)

        def visit_row(i, acc):
            for t in range(tiles):
                acc = visit(i, t, acc)
            return acc

        acc = lax.fori_loop(2, rows, visit_row, acc)

        @pl.when(more)
        def _():
            send_edge(k + 2, 1)

        if k < 2:
            sums[2 * k + 1] = acc[0]
            sums[2 * k + 2] = acc[1]

        @pl.when(k == 1)
        def _():
            send_parts(0, [sums[j] for j in range(5)])

        @pl.when(k == 2)
        def _():
            m = take_parts(0, 5)
            theta = m[1] / m[0]
            size = m[2] - theta * m[1]
            gain = jnp.maximum(size / m[0], 0.0)
            turn = m[3] - 2.0 * theta * m[2] + theta * theta * m[1]
            shift = jnp.where(size > 0.0, turn / jnp.where(size > 0.0, size, 1.0), 0.0)
            shift = jnp.minimum(jnp.maximum(shift, -1.0), 1.0)
            scalars[0] = theta
            scalars[1] = shift
            scalars[2] = gain
            for j, value in enumerate(gram_of(True)):
                sums[5 + j] = value

        return carry

    for k in range(STEPS):
        step(k, 0)
    theta, shift, gain = scalars[0], scalars[1], scalars[2]
    slope = -(shift + theta)
    bend = shift * theta - gain

    grams = gram_of(False)
    grams = [sums[5 + j] for j in range(len(early))] + list(grams)
    send_parts(1, grams)
    m = take_parts(1, len(pairs))
    gram = {}
    for (a, b), value in zip(pairs, m):
        gram[a, b] = gram[b, a] = value

    def times(p):
        out = [None] * 5
        def put(j, x):
            out[j] = x if out[j] is None else out[j] + x
        if p[0] is not None:
            put(0, theta * p[0])
            put(1, p[0])
        if p[1] is not None:
            put(0, gain * p[1])
            put(1, shift * p[1])
            put(2, p[1])
        if p[2] is not None:
            put(3, p[2])
        if p[3] is not None:
            put(4, p[3])
        return out

    def add(a, b, scale):
        out = []
        for x, y in zip(a, b):
            if y is None:
                out.append(x)
            elif x is None:
                out.append(scale * y)
            else:
                out.append(x + scale * y)
        return out

    def inner(a, b):
        total = None
        for i, x in enumerate(a):
            if x is None:
                continue
            line = None
            for j, y in enumerate(b):
                if y is not None:
                    term = gram[i, j] * y
                    line = term if line is None else line + term
            total = x * line if total is None else total + x * line
        return total

    one = jnp.ones((8, 128), jnp.float32)
    adj, res, way = [None] * 5, [one] + [None] * 4, [one] + [None] * 4
    norm = gram[0, 0]
    for step in range(STEPS):
        image = add(way, times(way), -one)
        alpha = norm / inner(way, image)
        adj = add(adj, way, alpha)
        res = add(res, image, -alpha)
        if step + 1 < STEPS:
            after = inner(res, res)
            way = add(res, way, after / norm)
            norm = after

    def back(q):
        q = [zero if x is None else x for x in q]
        return [
            q[0] - theta * q[1] + bend * q[2],
            q[1] + slope * q[2] + bend * q[3],
            q[2] + slope * q[3] + bend * q[4],
            q[3] + slope * q[4],
            q[4],
        ]

    adj_w = [wide(x) for x in back(adj)[:4]]
    res_w = [wide(x) for x in back(res)]

    def finish_row(i, carry):
        for t in range(tiles):
            at = pl.ds(PAD + 8 * t, 8)
            part = pl.ds(8 * t, 8)
            f = [fields[j, i, at, :] for j in range(1, STEPS + 2)]
            x = adj_w[0] * f[0]
            for j in range(1, 4):
                x += adj_w[j] * f[j]
            r = res_w[0] * f[0]
            for j in range(1, 5):
                r += res_w[j] * f[j]
            adjoint_ref[i - 1, part, :] = x
            residual_ref[i - 1, part, :] = r * diag[i - 1, part, :]
        return carry

    lax.fori_loop(1, rows + 1, finish_row, 0)

    def left(k, carry):
        for group in (0, 1):
            edge_copy(k, group).wait_send()

        def one(side, carry):
            @pl.when(has(side))
            def _():
                for c in range(cuts):
                    row_copy(k, side, c).wait_send()

            return carry

        return lax.fori_loop(0, 2, one, carry)

    lax.fori_loop(0, STEPS + 1, left, 0)

    def sent(offset, carry):
        for which in (0, 1):
            part_copy(which, offset).wait_send()
        return carry

    lax.fori_loop(1, n, sent, 0)


def per_device(ngx, ngy, cuts, temp, label, flag, source, k0, tc, ts):
    rows, cols, depth = temp.shape
    n = ngx * ngy
    block = lambda dtype: pltpu.VMEM((rows, cols, depth), dtype)
    padded = pltpu.VMEM((STEPS + 2, rows + 2, cols + 2 * PAD, depth), jnp.float32)
    f32 = jnp.float32
    out = jax.ShapeDtypeStruct((rows, cols, depth), f32)
    dma = pltpu.SemaphoreType.DMA
    return pl.pallas_call(
        functools.partial(kernel, ngx, ngy, cuts),
        out_shape=(out, out),
        in_specs=[pl.BlockSpec(memory_space=pltpu.HBM)] * 7,
        out_specs=(pl.BlockSpec(memory_space=pltpu.VMEM),) * 2,
        scratch_shapes=[pltpu.SMEM(k0.shape, f32)] * 3
        + [block(f32), block(jnp.int32), block(jnp.int32), block(f32)]
        + [padded, pltpu.VMEM((3, 8, 128), f32), pltpu.VMEM((15, 8, 128), f32)]
        + [pltpu.VMEM((rows + 1, cols, depth), f32)]
        + [block(f32)] * 6
        + [
            pltpu.VMEM((STEPS + 1, 16, depth), f32),
            pltpu.VMEM((STEPS + 1, 16, depth), f32),
            pltpu.VMEM((2, 8, 128), f32),
            pltpu.VMEM((2, n, 8, 128), f32),
            dma((4, 3)),
            dma((3,)),
            dma((STEPS + 1, 2, cuts)),
            dma((STEPS + 1, 2, cuts)),
            dma((STEPS + 1, 2)),
            dma((STEPS + 1, 2)),
            dma((2, n)),
            dma((2, n)),
        ],
        compiler_params=pltpu.CompilerParams(
            collective_id=0, has_side_effects=True, vmem_limit_bytes=62 * 1024 * 1024
        ),
    )(temp, label, flag, source, k0, tc, ts)


def solution(mesh):
    block = P(("cycle", "gx"), "gy", None)
    shared = P("gx", "gy", None)
    return jax.shard_map(
        functools.partial(per_device, mesh.shape["gx"], mesh.shape["gy"], 4),
        mesh=mesh,
        in_specs=(block, shared, shared, block, P(), P(), P()),
        out_specs=(block, block),
        check_vma=False,
    )
```
